128 devices in a mesh: dp: 16 (over z, y_lo, core), fsdp: 8 (over x, y_hi).
Axes of the slice: x: 4, y: 4 (y_hi: 2, y_lo: 2; y = y_hi * 2 + y_lo), z: 4, core: 2. Of those that a mesh axis runs over, the one named last changes fastest.
Arguments:
- pooled: bfloat16 [16384, 1152], P(('dp', 'fsdp')), may hold values from -6 to 6
- text_feats: bfloat16 [16384, 1152], P(('dp', 'fsdp')), may hold values from -6 to 6
- out_weight: bfloat16 [1152, 1152], P('fsdp'), may hold values from -0.1875 to 0.1875
- logit_scale: float32 [1], replicated, may hold values from 8 to 12
- logit_bias: float32 [1], replicated, may hold values from -7 to -4
Outputs:
- grad_text: float32 [16384, 1152], P(('dp', 'fsdp'))
- grad_pooled: bfloat16 [16384, 1152], P(('dp', 'fsdp'))
- grad_weight: float32 [1152, 1152], P('fsdp')
The draws below stay inside these ranges and needn't reach their ends.
All inputs are finite; a program needn't handle non-finite values.
Results may differ from the reference program's by a relative error of at most 0.028.
Values may be sent and summed in bfloat16 or wider, within the bound.
No kernel may reach another device: no remote copies, remote signals or barrier semaphores. Data moves between devices by JAX's collectives and lax.ppermute only.
A program may use at most 128 MiB of HBM per device.

```python
import math
import jax
import jax.numpy as jnp
from jax import lax

D = 1152
GROUP = 1024
BATCH = 16384


def block_scale(stream_key, shape, split, low, top_value):
    level = 1.0
    for axis_at, blocks in split:
        steps = jax.random.uniform(jax.random.fold_in(jax.random.fold_in(stream_key, 6), axis_at), (blocks,), jnp.float32, low / len(split), top_value / len(split))
        level = level * jnp.repeat(jnp.exp(steps), shape[axis_at] // blocks).reshape((-1,) + (1,) * (len(shape) - 1 - axis_at))
    return level


def scatter_about(stream_key, shape, width, reach, pieces=(), held_as=jnp.bfloat16):
    array = width * jax.random.normal(stream_key, shape, jnp.float32)
    if pieces:
        array = array * block_scale(stream_key, shape, pieces, -0.22, 0.18)
    return jnp.clip(array, -reach, reach).astype(held_as)


def setup_inputs(seed: int = 0) -> dict:
    seeds = jax.random.split(jax.random.key(seed), 6)
    return {
        "pooled": scatter_about(seeds[0], (BATCH, D), 1.0, 6.0, ((0, 128),)),
        "text_feats": scatter_about(seeds[1], (BATCH, D), 1.0, 6.0, ((0, 128),)),
        "out_weight": scatter_about(seeds[2], (D, D), D ** -0.5, 0.1875, ((0, 8),)),
        "logit_scale": jnp.clip(jnp.exp(jax.random.uniform(seeds[3], (1,), jnp.float32, math.log(8.0), math.log(12.0))), 8.0, 12.0),
        "logit_bias": jnp.clip(jax.random.uniform(seeds[4], (1,), jnp.float32, -7.0, -4.0), -7.0, -4.0),
    }


epsilon = 1e-06

def unit_rows(values):
    norms = jnp.sqrt(lax.optimization_barrier(jnp.sum(values * values, axis=-1, keepdims=True)) + epsilon)
    return (values / norms, norms)

def unit_backward(upstream, unit, norms):
    return (upstream - unit * lax.optimization_barrier(jnp.sum(unit * upstream, axis=-1, keepdims=True))) / norms

def reference(pooled, text_feats, out_weight, logit_scale, logit_bias):
    logit_mult = logit_scale[0]
    logit_shift = logit_bias[0]
    batch_rows = pooled.shape[0]
    feat_dim = pooled.shape[1]
    image_raw = jnp.dot(pooled, out_weight, preferred_element_type=jnp.float32)
    image_unit, image_norm = unit_rows(image_raw)
    image_emb = image_unit.astype(jnp.bfloat16)
    text_unit, text_norm = unit_rows(text_feats.astype(jnp.float32))
    text_emb = text_unit.astype(jnp.bfloat16)
    block_rows = GROUP
    block_count = batch_rows // block_rows
    image_blocks = image_emb.reshape(block_count, block_rows, feat_dim)
    text_ids = jnp.arange(batch_rows, dtype=jnp.int32)

    def scan_block(text_grad, block_item):
        block_index, block_images = block_item
        logits = logit_mult * jnp.dot(block_images, text_emb.T, preferred_element_type=jnp.float32) + logit_shift
        image_ids = block_index * block_rows + jnp.arange(block_rows, dtype=jnp.int32)
        pair_sign = jnp.where(image_ids[:, None] == text_ids[None, :], 1.0, -1.0)
        pair_grad = (-pair_sign * jax.nn.sigmoid(-pair_sign * logits) * logit_mult).astype(jnp.bfloat16)
        block_grad = jnp.dot(pair_grad, text_emb, preferred_element_type=jnp.float32)
        text_grad = text_grad + jnp.dot(pair_grad.T, block_images, preferred_element_type=jnp.float32)
        return (text_grad, block_grad)
    start_grad = jnp.zeros((batch_rows, feat_dim), jnp.float32)
    text_grad, image_grad = lax.scan(scan_block, start_grad, (jnp.arange(block_count, dtype=jnp.int32), image_blocks))
    image_grad = image_grad.reshape(batch_rows, feat_dim)
    grad_text = unit_backward(text_grad, text_unit, text_norm)
    raw_grad = unit_backward(image_grad, image_unit, image_norm).astype(jnp.bfloat16)
    grad_pooled = jnp.dot(raw_grad, out_weight.T, preferred_element_type=jnp.float32).astype(jnp.bfloat16)
    grad_weight = jnp.dot(pooled.T, raw_grad, preferred_element_type=jnp.float32)
    return (grad_text, grad_pooled, grad_weight)
```

```python
import functools

import jax
import jax.numpy as jnp
from jax import lax
from jax.experimental import pallas as pl
from jax.experimental.pallas import tpu as pltpu
from jax.sharding import PartitionSpec as P

epsilon = 1e-06
BF = jnp.bfloat16
F32 = jnp.float32
AXES = ("dp", "fsdp")
SIZES = {"z": 4, "yl": 2, "c": 2, "x": 4, "yh": 2}


def place_of(i):
    dp, fs = divmod(i, 8)
    return {"z": dp // 4, "yl": dp // 2 % 2, "c": dp % 2, "x": fs // 2, "yh": fs % 2}


def index_of(p):
    return (p["z"] * 4 + p["yl"] * 2 + p["c"]) * 8 + p["x"] * 2 + p["yh"]


def shift(value, axis, by):
    pairs = []
    for i in range(128):
        p = place_of(i)
        p[axis] = (p[axis] + by) % SIZES[axis]
        pairs.append((i, index_of(p)))
    return lax.ppermute(value, AXES, pairs)


def ring_gather(block, axis):
    half = block.shape[0] // 2
    from_minus = shift(block, axis, 1)
    from_plus = shift(block, axis, -1)
    far_a = shift(from_minus[:half], axis, 1)
    far_b = shift(from_plus[half:], axis, -1)
    return [block, from_plus, far_a, far_b, from_minus]


def ring_scatter(blocks, axis):
    half = blocks[0].shape[0] // 2
    far = blocks[2].astype(BF)
    a = shift(far[:half], axis, 1).astype(F32)
    b = shift(far[half:], axis, -1).astype(F32)
    plus = blocks[1]
    minus = blocks[3]
    plus = jnp.concatenate([plus[:half] + a, plus[half:]], 0).astype(BF)
    minus = jnp.concatenate([minus[:half], minus[half:] + b], 0).astype(BF)
    r1 = shift(plus, axis, 1).astype(F32)
    r2 = shift(minus, axis, -1).astype(F32)
    return blocks[0] + (r1 + r2)


def unit_rows(values):
    norms = jnp.sqrt(jnp.sum(values * values, axis=-1, keepdims=True) + epsilon)
    return (values / norms, norms)


def unit_backward(upstream, unit, norms):
    return (upstream - unit * jnp.sum(unit * upstream, axis=-1, keepdims=True)) / norms


def weight_rows(starts):
    return [(dx, dy, starts[0], starts[1]) for dx in range(4) for dy in range(2)]


def block_row(pos, dx, dy):
    x, yh = pos[0], pos[1]
    return (lax.rem(x + dx, 4) * 2 + lax.rem(yh + dy, 2)) * 144


def assemble_kernel(pos, own, oth, out, sem):
    c = pos[2]
    copies = []
    for dx in range(4):
        for dy in range(2):
            k = dx * 2 + dy
            base = block_row(pos, dx, dy)
            copies.append(pltpu.make_async_copy(
                own.at[pl.ds(k * 80, 80)],
                out.at[pl.ds(pl.multiple_of(base + c * 64, 16), 80)], sem.at[2 * k]))
            copies.append(pltpu.make_async_copy(
                oth.at[pl.ds(pl.multiple_of(k * 80 + 16 * (1 - c), 16), 64)],
                out.at[pl.ds(pl.multiple_of(base + 80 * (1 - c), 16), 64)], sem.at[2 * k + 1]))
    for cp in copies:
        cp.start()
    for cp in copies:
        cp.wait()


def assemble(pos, own, oth):
    return pl.pallas_call(
        assemble_kernel,
        out_shape=jax.ShapeDtypeStruct((1152, 1152), BF),
        in_specs=[pl.BlockSpec(memory_space=pltpu.SMEM), pl.BlockSpec(memory_space=pl.ANY), pl.BlockSpec(memory_space=pl.ANY)],
        out_specs=pl.BlockSpec(memory_space=pl.ANY),
        scratch_shapes=[pltpu.SemaphoreType.DMA((16,))],
    )(pos, own, oth)


def spread_kernel(pos, whole, keep, send, sem):
    c = pos[2]
    copies = []
    for dx in range(4):
        for dy in range(2):
            k = dx * 2 + dy
            base = block_row(pos, dx, dy)
            copies.append(pltpu.make_async_copy(
                whole.at[pl.ds(pl.multiple_of(base + c * 64, 16), 80)],
                keep.at[pl.ds(k * 80, 80)], sem.at[2 * k]))
            copies.append(pltpu.make_async_copy(
                whole.at[pl.ds(pl.multiple_of(base + (1 - c) * 64, 16), 80)],
                send.at[pl.ds(k * 80, 80)], sem.at[2 * k + 1]))
    for cp in copies:
        cp.start()
    for cp in copies:
        cp.wait()


def spread(pos, whole):
    return pl.pallas_call(
        spread_kernel,
        out_shape=[jax.ShapeDtypeStruct((640, 1152), BF)] * 2,
        in_specs=[pl.BlockSpec(memory_space=pltpu.SMEM), pl.BlockSpec(memory_space=pl.ANY)],
        out_specs=[pl.BlockSpec(memory_space=pl.ANY)] * 2,
        scratch_shapes=[pltpu.SemaphoreType.DMA((16,))],
    )(pos, whole)


def local(pooled, text_feats, out_weight, logit_scale, logit_bias):
    dp = lax.axis_index("dp")
    fs = lax.axis_index("fsdp")
    core = dp % 2
    pos = jnp.stack([fs // 2, fs % 2, core]).astype(jnp.int32)
    mult = logit_scale[0]
    bias = logit_bias[0]

    wq = lax.dynamic_slice_in_dim(out_weight, core * 64, 80, 0)
    wy = shift(wq, "yh", 1)
    w_parts = ring_gather(jnp.concatenate([wq, wy], 0), "x")
    w_own = jnp.concatenate([w_parts[0], w_parts[1], w_parts[2], w_parts[3], w_parts[4]], 0)
    w_oth = shift(w_own, "c", 1)
    weight = assemble(pos, w_own, w_oth)

    pooled_y = shift(pooled, "yh", 1)
    i0 = jnp.concatenate(ring_gather(pooled, "x"), 0)
    i1 = jnp.concatenate(ring_gather(pooled_y, "x"), 0)

    text_unit, text_norm = unit_rows(text_feats.astype(F32))
    text_emb = text_unit.astype(BF)
    text_y = shift(text_emb, "yl", 1)
    t0 = jnp.concatenate(ring_gather(text_emb, "z"), 0)
    t1 = jnp.concatenate(ring_gather(text_y, "z"), 0)
    t0 = jnp.concatenate([t0, shift(t0, "c", 1)], 0)
    t1 = jnp.concatenate([t1, shift(t1, "c", 1)], 0)

    def embed(rows):
        raw = jnp.dot(rows, weight, preferred_element_type=F32)
        unit, norm = unit_rows(raw)
        return unit.astype(BF), norm

    e0, n0 = embed(i0)
    e1, n1 = embed(i1)

    def pair(e, t, diagonal):
        logits = mult * lax.dot_general(e, t, (((1,), (1,)), ((), ())), preferred_element_type=F32) + bias
        if diagonal:
            row = lax.broadcasted_iota(jnp.int32, logits.shape, 0)
            col = lax.broadcasted_iota(jnp.int32, logits.shape, 1)
            sign = jnp.where((row == col) & (row < 128), 1.0, -1.0)
            return (-sign * jax.nn.sigmoid(-sign * logits) * mult).astype(BF)
        return (jax.nn.sigmoid(logits) * mult).astype(BF)

    def back_t(pg, e):
        return lax.dot_general(pg, e, (((0,), (0,)), ((), ())), preferred_element_type=F32)

    def project(g, e, n):
        return unit_backward(g, e.astype(F32), n)

    pg00 = pair(e0, t0, True)
    pg01 = pair(e0, t1, False)
    g0 = jnp.dot(pg00, t0, preferred_element_type=F32) + jnp.dot(pg01, t1, preferred_element_type=F32)
    r0 = project(g0, e0, n0)
    pg11 = pair(e1, t1, False)
    gt1 = back_t(pg01, e0) + back_t(pg11, e1)
    pg10 = pair(e1, t0, False)
    g1 = jnp.dot(pg11, t1, preferred_element_type=F32) + jnp.dot(pg10, t0, preferred_element_type=F32)
    r1 = project(g1, e1, n1)
    gt0 = back_t(pg00, e0) + back_t(pg10, e1)

    def split4(v):
        return [v[k * 128:(k + 1) * 128] for k in range(4)]

    def text_sum(g):
        other = shift(g[512:].astype(BF), "c", 1).astype(F32)
        return ring_scatter(split4(g[:512] + other), "z")

    text_1 = text_sum(gt1)
    text_0 = text_sum(gt0)
    text_grad = text_0 + shift(text_1.astype(BF), "yl", 1).astype(F32)
    grad_text = unit_backward(text_grad, text_unit, text_norm)

    image_1 = ring_scatter(split4(r1), "x")
    image_0 = ring_scatter(split4(r0), "x")
    raw_grad = (image_0 + shift(image_1.astype(BF), "yh", 1).astype(F32)).astype(BF)
    grad_pooled = lax.dot_general(raw_grad, weight, (((1,), (1,)), ((), ())), preferred_element_type=F32).astype(BF)

    gw = (back_t(i0, r0.astype(BF)) + back_t(i1, r1.astype(BF))).astype(BF)
    keep, send = spread(pos, gw)
    s = keep.astype(F32) + shift(send, "c", 1).astype(F32)
    s = ring_scatter([s[k * 160:(k + 1) * 160] for k in range(4)], "x")
    s = (s[:80] + shift(s[80:].astype(BF), "yh", 1).astype(F32)).astype(BF)
    zp, zm, zf = shift(s, "z", 1), shift(s, "z", -1), shift(s, "z", 2)
    s = ((s.astype(F32) + zf.astype(F32)) + (zp.astype(F32) + zm.astype(F32))).astype(BF)
    s = (s.astype(F32) + shift(s, "yl", 1).astype(F32)).astype(BF)
    o = shift(s, "c", 1)
    lo = jnp.where(core == 0, s, o)
    hi = jnp.where(core == 0, o, s)
    grad_weight = jnp.concatenate([lo, hi[16:]], 0).astype(F32)
    return (grad_text, grad_pooled, grad_weight)


def solution(mesh):
    placed = (P(AXES, None), P(AXES, None), P("fsdp", None), P(), P())
    return jax.shard_map(
        local,
        mesh=mesh,
        in_specs=placed,
        out_specs=(P(AXES, None), P(AXES, None), P("fsdp", None)),
        check_vma=False,
    )
```

```python
import functools

import jax
import jax.numpy as jnp
from jax import lax
from jax.experimental import pallas as pl
from jax.experimental.pallas import tpu as pltpu
from jax.sharding import PartitionSpec as P

epsilon = 1e-06
BF = jnp.bfloat16
F32 = jnp.float32
AXES = ("dp", "fsdp")
SIZES = {"z": 4, "yl": 2, "c": 2, "x": 4, "yh": 2}


def place_of(i):
    dp, fs = divmod(i, 8)
    return {"z": dp // 4, "yl": dp // 2 % 2, "c": dp % 2, "x": fs // 2, "yh": fs % 2}


def index_of(p):
    return (p["z"] * 4 + p["yl"] * 2 + p["c"]) * 8 + p["x"] * 2 + p["yh"]


def shift(value, axis, by):
    pairs = []
    for i in range(128):
        p = place_of(i)
        p[axis] = (p[axis] + by) % SIZES[axis]
        pairs.append((i, index_of(p)))
    return lax.ppermute(value, AXES, pairs)


def after(value, *others):
    return lax.optimization_barrier((value,) + others)[0]


def ring(block, axis):
    half = block.shape[0] // 2
    minus = shift(block, axis, 1)
    plus = shift(block, axis, -1)
    far_a = shift(minus[:half], axis, 1)
    far_b = shift(plus[half:], axis, -1)
    return plus, minus, far_a, far_b


def rows_of(v, k, n=128):
    return v[k * n:(k + 1) * n]


def ring_sum(v, axis, n=128):
    half = n // 2
    far = rows_of(v, 2, n).astype(BF)
    a = shift(far[:half], axis, 1).astype(F32)
    b = shift(far[half:], axis, -1).astype(F32)
    plus, minus = rows_of(v, 1, n), rows_of(v, 3, n)
    plus = jnp.concatenate([plus[:half] + a, plus[half:]], 0).astype(BF)
    minus = jnp.concatenate([minus[:half], minus[half:] + b], 0).astype(BF)
    r1 = shift(plus, axis, 1).astype(F32)
    r2 = shift(minus, axis, -1).astype(F32)
    return rows_of(v, 0, n) + (r1 + r2)


def unit_rows(values):
    norms = jnp.sqrt(jnp.sum(values * values, axis=-1, keepdims=True) + epsilon)
    return (values / norms, norms)


def unit_backward(upstream, unit, norms):
    return (upstream - unit * jnp.sum(unit * upstream, axis=-1, keepdims=True)) / norms


def block_row(pos, dx, dy):
    x, yh = pos[0], pos[1]
    return (lax.rem(x + dx, 4) * 2 + lax.rem(yh + dy, 2)) * 144


def assemble_kernel(pos, own, oth, out):
    c = pos[2]
    for dx in range(4):
        for dy in range(2):
            k = (dx * 2 + dy) * 80
            base = block_row(pos, dx, dy)
            out[pl.ds(pl.multiple_of(base + c * 64, 16), 80), :] = own[pl.ds(k, 80), :]
            out[pl.ds(pl.multiple_of(base + 80 * (1 - c), 16), 64), :] = oth[pl.ds(pl.multiple_of(k + 16 * (1 - c), 16), 64), :]


def assemble(pos, *parts):
    return pl.pallas_call(
        assemble_kernel,
        out_shape=jax.ShapeDtypeStruct((1152, 1152), BF),
        in_specs=[pl.BlockSpec(memory_space=pltpu.SMEM)] + [pl.BlockSpec(memory_space=pltpu.VMEM)] * 2,
        out_specs=pl.BlockSpec(memory_space=pltpu.VMEM),
        compiler_params=pltpu.CompilerParams(vmem_limit_bytes=32 * 2**20),
    )(pos, *parts)


def spread_kernel(pos, whole, keep, send):
    c = pos[2]
    for dx in range(4):
        for dy in range(2):
            k = dx * 2 + dy
            base = block_row(pos, dx, dy)
            keep[pl.ds(k * 80, 80), :] = whole[pl.ds(pl.multiple_of(base + c * 64, 16), 80), :]
            send[pl.ds(k * 80, 80), :] = whole[pl.ds(pl.multiple_of(base + (1 - c) * 64, 16), 80), :]


def spread(pos, whole):
    return pl.pallas_call(
        spread_kernel,
        out_shape=[jax.ShapeDtypeStruct((640, 1152), BF)] * 2,
        in_specs=[pl.BlockSpec(memory_space=pltpu.SMEM), pl.BlockSpec(memory_space=pltpu.VMEM)],
        out_specs=[pl.BlockSpec(memory_space=pltpu.VMEM)] * 2,
        compiler_params=pltpu.CompilerParams(vmem_limit_bytes=32 * 2**20),
    )(pos, whole)


def local(pooled, text_feats, out_weight, logit_scale, logit_bias):
    dp = lax.axis_index("dp")
    fs = lax.axis_index("fsdp")
    core = dp % 2
    pos = jnp.stack([fs // 2, fs % 2, core]).astype(jnp.int32)
    mult = logit_scale[0]
    bias = logit_bias[0]

    wq = lax.dynamic_slice_in_dim(out_weight, core * 64, 80, 0)
    wy = shift(wq, "yh", 1)
    pooled_y = shift(pooled, "yh", 1)
    own = jnp.concatenate([wq, wy, pooled], 0)
    plus, minus, fa, fb = ring(own, "x")
    w_own = jnp.concatenate([own[:160], plus[:160], fa, fb[:16], minus[:160]], 0)
    i0 = jnp.concatenate([pooled, plus[160:], fb[16:], minus[160:]], 0)
    weight = assemble(pos, w_own, shift(w_own, "c", 1))
    plus, minus, fa, fb = ring(pooled_y, "x")
    i1 = jnp.concatenate([pooled_y, plus, fa, fb, minus], 0)

    text_unit, text_norm = unit_rows(text_feats.astype(F32))
    text_emb = text_unit.astype(BF)
    text_2 = jnp.concatenate([text_emb, shift(text_emb, "yl", 1)], 0)
    plus, minus, fa, fb = ring(text_2, "z")
    texts = jnp.concatenate([text_2, plus, fa, fb, minus], 0)
    texts = jnp.concatenate([texts, shift(texts, "c", 1)], 0)

    def embed(rows):
        raw = jnp.dot(rows, weight, preferred_element_type=F32)
        unit, norm = unit_rows(raw)
        return unit.astype(BF), norm

    e0, n0 = embed(i0)
    e1, n1 = embed(i1)

    def pair(e, t):
        logits = mult * lax.dot_general(e, t, (((1,), (1,)), ((), ())), preferred_element_type=F32) + bias
        return (jax.nn.sigmoid(logits) * mult).astype(BF)

    def pair_own(e, t):
        logits = mult * lax.dot_general(e, t, (((1,), (1,)), ((), ())), preferred_element_type=F32) + bias
        row = lax.broadcasted_iota(jnp.int32, logits.shape, 0)
        col = lax.broadcasted_iota(jnp.int32, logits.shape, 1)
        sign = jnp.where(row == col, 1.0, -1.0)
        return (-sign * jax.nn.sigmoid(-sign * logits) * mult).astype(BF)

    def back_t(pg, e):
        return lax.dot_general(pg, e, (((0,), (0,)), ((), ())), preferred_element_type=F32)

    def project(g, e, n):
        return unit_backward(g, e.astype(F32), n)

    pg1 = pair(e1, texts)
    r1 = project(jnp.dot(pg1, texts, preferred_element_type=F32), e1, n1)
    r1b = r1.astype(BF)
    image_1 = ring_sum(r1, "x").astype(BF)
    pg0 = lax.dynamic_update_slice(pair(e0, texts), pair_own(e0[:128], texts[:128]), (0, 0))
    r0 = project(jnp.dot(pg0, texts, preferred_element_type=F32), e0, n0)
    r0b = r0.astype(BF)

    gw = (back_t(i0, r0b) + back_t(i1, r1b)).astype(BF)
    gw = after(gw, image_1)
    keep, send = spread(pos, gw)
    s = keep.astype(F32) + shift(send, "c", 1).astype(F32)
    s = ring_sum(s, "x", 160)
    r0 = after(r0, s)
    s = (s[:80] + shift(s[80:].astype(BF), "yh", 1).astype(F32)).astype(BF)
    zp, zm, zf = shift(s, "z", 1), shift(s, "z", -1), shift(s, "z", 2)
    s = ((s.astype(F32) + zf.astype(F32)) + (zp.astype(F32) + zm.astype(F32))).astype(BF)
    s = (s.astype(F32) + shift(s, "yl", 1).astype(F32)).astype(BF)
    o = shift(s, "c", 1)
    lo = jnp.where(core == 0, s, o)
    hi = jnp.where(core == 0, o, s)
    grad_weight = jnp.concatenate([lo, hi[16:]], 0).astype(F32)

    gt = back_t(pg0, e0) + back_t(pg1, e1)
    gt = gt[:1024] + shift(gt[1024:].astype(BF), "c", 1).astype(F32)
    gt = ring_sum(gt, "z", 256)
    text_grad = gt[:128] + shift(gt[128:].astype(BF), "yl", 1).astype(F32)
    grad_text = unit_backward(text_grad, text_unit, text_norm)

    image_0 = ring_sum(r0, "x")
    raw_grad = (image_0 + shift(image_1, "yh", 1).astype(F32)).astype(BF)
    grad_pooled = lax.dot_general(raw_grad, weight, (((1,), (1,)), ((), ())), preferred_element_type=F32).astype(BF)
    return (grad_text, grad_pooled, grad_weight)


def solution(mesh):
    placed = (P(AXES, None), P(AXES, None), P("fsdp", None), P(), P())
    return jax.shard_map(
        local,
        mesh=mesh,
        in_specs=placed,
        out_specs=(P(AXES, None), P(AXES, None), P("fsdp", None)),
        check_vma=False,
    )
```

```python
import functools

import jax
import jax.numpy as jnp
from jax import lax
from jax.experimental import pallas as pl
from jax.experimental.pallas import tpu as pltpu
from jax.sharding import PartitionSpec as P

epsilon = 1e-06
BF = jnp.bfloat16
F32 = jnp.float32
AXES = ("dp", "fsdp")
SIZES = {"z": 4, "yl": 2, "c": 2, "x": 4, "yh": 2}


def place_of(i):
    dp, fs = divmod(i, 8)
    return {"z": dp // 4, "yl": dp // 2 % 2, "c": dp % 2, "x": fs // 2, "yh": fs % 2}


def index_of(p):
    return (p["z"] * 4 + p["yl"] * 2 + p["c"]) * 8 + p["x"] * 2 + p["yh"]


def shift(value, axis, by):
    pairs = []
    for i in range(128):
        p = place_of(i)
        p[axis] = (p[axis] + by) % SIZES[axis]
        pairs.append((i, index_of(p)))
    return lax.ppermute(value, AXES, pairs)


def join(*values):
    return lax.optimization_barrier(values)


def both_ways(block, axis):
    return shift(block, axis, -1), shift(block, axis, 1)


def rows_of(v, k, n=128):
    return v[k * n:(k + 1) * n]


def ring_first(v, axis):
    half = v[0].shape[0] // 2
    far = v[2].astype(BF)
    a = shift(far[:half], axis, 1).astype(F32)
    b = shift(far[half:], axis, -1).astype(F32)
    plus = jnp.concatenate([v[1][:half] + a, v[1][half:]], 0).astype(BF)
    minus = jnp.concatenate([v[3][:half], v[3][half:] + b], 0).astype(BF)
    return v[0], plus, minus


def ring_second(own, plus, minus, axis):
    return own + (shift(plus, axis, 1).astype(F32) + shift(minus, axis, -1).astype(F32))


def near_sum(v, axis, n=128):
    r1 = shift(rows_of(v, 1, n).astype(BF), axis, 1).astype(F32)
    r2 = shift(rows_of(v, 2, n).astype(BF), axis, 2).astype(F32)
    r3 = shift(rows_of(v, 3, n).astype(BF), axis, -1).astype(F32)
    return (rows_of(v, 0, n) + r2) + (r1 + r3)


def unit_rows(values):
    norms = jnp.sqrt(jnp.sum(values * values, axis=-1, keepdims=True) + epsilon)
    return (values / norms, norms)


def unit_backward(upstream, unit, norms):
    return (upstream - unit * jnp.sum(unit * upstream, axis=-1, keepdims=True)) / norms


def block_row(pos, dx, dy):
    x, yh = pos[0], pos[1]
    return (lax.rem(x + dx, 4) * 2 + lax.rem(yh + dy, 2)) * 144


def prepare_kernel(pos, weight, pooled, text, own, emb):
    own[pl.ds(0, 80), :] = weight[pl.ds(pl.multiple_of(pos[2] * 64, 16), 80), :]
    own[pl.ds(80, 128), :] = pooled[...]
    values = text[...].astype(F32)
    emb[...] = (values / jnp.sqrt(jnp.sum(values * values, axis=-1, keepdims=True) + epsilon)).astype(BF)


def prepare(pos, weight, pooled, text):
    return pl.pallas_call(
        prepare_kernel,
        out_shape=[jax.ShapeDtypeStruct((208, 1152), BF), jax.ShapeDtypeStruct((128, 1152), BF)],
        in_specs=[pl.BlockSpec(memory_space=pltpu.SMEM)] + [pl.BlockSpec(memory_space=pltpu.VMEM)] * 3,
        out_specs=[pl.BlockSpec(memory_space=pltpu.VMEM)] * 2,
        compiler_params=pltpu.CompilerParams(vmem_limit_bytes=32 * 2**20),
    )(pos, weight, pooled, text)


def assemble_kernel(pos, near, far, near_c, far_c, out):
    c = pos[2]
    for dx in range(4):
        for dy in range(2):
            own, oth, k = (far, far_c, 96 * dy) if dx == 2 else (near, near_c, ((0, 1, 2, 2)[dx] * 2 + dy) * 80)
            base = block_row(pos, dx, dy)
            out[pl.ds(pl.multiple_of(base + c * 64, 16), 80), :] = own[pl.ds(k, 80), :]
            out[pl.ds(pl.multiple_of(base + 80 * (1 - c), 16), 64), :] = oth[pl.ds(pl.multiple_of(k + 16 * (1 - c), 16), 64), :]


def assemble(pos, *parts):
    return pl.pallas_call(
        assemble_kernel,
        out_shape=jax.ShapeDtypeStruct((1152, 1152), BF),
        in_specs=[pl.BlockSpec(memory_space=pltpu.SMEM)] + [pl.BlockSpec(memory_space=pltpu.VMEM)] * 4,
        out_specs=pl.BlockSpec(memory_space=pltpu.VMEM),
        compiler_params=pltpu.CompilerParams(vmem_limit_bytes=32 * 2**20),
    )(pos, *parts)


def spread_kernel(pos, whole, keep, send):
    c = pos[2]
    for dx in range(4):
        for dy in range(2):
            k = dx * 2 + dy
            base = block_row(pos, dx, dy)
            keep[pl.ds(k * 80, 80), :] = whole[pl.ds(pl.multiple_of(base + c * 64, 16), 80), :]
            send[pl.ds(k * 80, 80), :] = whole[pl.ds(pl.multiple_of(base + (1 - c) * 64, 16), 80), :]


def spread(pos, whole):
    return pl.pallas_call(
        spread_kernel,
        out_shape=[jax.ShapeDtypeStruct((640, 1152), BF)] * 2,
        in_specs=[pl.BlockSpec(memory_space=pltpu.SMEM), pl.BlockSpec(memory_space=pltpu.VMEM)],
        out_specs=[pl.BlockSpec(memory_space=pltpu.VMEM)] * 2,
        compiler_params=pltpu.CompilerParams(vmem_limit_bytes=32 * 2**20),
    )(pos, whole)


def local(pooled, text_feats, out_weight, logit_scale, logit_bias):
    dp = lax.axis_index("dp")
    fs = lax.axis_index("fsdp")
    core = dp % 2
    pos = jnp.stack([fs // 2, fs % 2, core]).astype(jnp.int32)
    mult = logit_scale[0]
    bias = logit_bias[0]

    own, text_emb = prepare(pos, out_weight, pooled, text_feats)
    oth = shift(own, "yh", 1)
    own_p, own_m = both_ways(own, "x")
    oth_p, oth_m = both_ways(oth, "x")
    far_a = shift(jnp.concatenate([own_m[:96], oth_m[:96]], 0), "x", 1)
    far_b = shift(jnp.concatenate([own_p[96:], oth_p[96:]], 0), "x", -1)
    w_near = jnp.concatenate([v[:80] for v in (own, oth, own_p, oth_p, own_m, oth_m)], 0)
    w_far_c = shift(far_a, "c", 1)
    weight = assemble(pos, w_near, far_a, shift(w_near, "c", 1), w_far_c)
    i0 = jnp.concatenate([pooled, own_p[80:], far_a[80:96], far_b[:112], own_m[80:]], 0)
    i1 = jnp.concatenate([oth[80:], oth_p[80:], far_a[176:], far_b[112:], oth_m[80:]], 0)

    text_own, _ = join(text_emb, oth)
    text_oth = shift(text_own, "yl", 1)
    t_p, t_m = both_ways(text_emb, "z")
    u_p, u_m = both_ways(text_oth, "z")
    fa = shift(jnp.concatenate([t_m[:64], u_m[:64]], 0), "z", 1)
    fb = shift(jnp.concatenate([t_p[64:], u_p[64:]], 0), "z", -1)
    t_near = jnp.concatenate([text_emb, text_oth, t_p, u_p, t_m, u_m], 0)
    t_far = jnp.concatenate([fa[:64], fb[:64], fa[64:], fb[64:]], 0)
    t_near, t_far, _ = join(t_near, t_far, w_far_c)
    c_near = shift(t_near, "c", 1)
    c_far = shift(t_far, "c", 1)
    texts = jnp.concatenate([t_near[:512], t_far, t_near[512:], c_near[:512], c_far, c_near[512:]], 0)

    def embed(rows):
        raw = jnp.dot(rows, weight, preferred_element_type=F32)
        unit, norm = unit_rows(raw)
        return unit.astype(BF), norm

    e1, n1 = embed(i1)
    e0, n0 = embed(i0)

    def pair(e, t):
        logits = mult * lax.dot_general(e, t, (((1,), (1,)), ((), ())), preferred_element_type=F32) + bias
        return (jax.nn.sigmoid(logits) * mult).astype(BF)

    def pair_own(e, t):
        logits = mult * lax.dot_general(e, t, (((1,), (1,)), ((), ())), preferred_element_type=F32) + bias
        row = lax.broadcasted_iota(jnp.int32, logits.shape, 0)
        col = lax.broadcasted_iota(jnp.int32, logits.shape, 1)
        sign = jnp.where(row == col, 1.0, -1.0)
        return (-sign * jax.nn.sigmoid(-sign * logits) * mult).astype(BF)

    def back_t(pg, e):
        return lax.dot_general(pg, e, (((0,), (0,)), ((), ())), preferred_element_type=F32)

    def project(g, e, n):
        return unit_backward(g, e.astype(F32), n)

    pg1 = pair(e1, texts)
    r1 = project(jnp.dot(pg1, texts, preferred_element_type=F32), e1, n1)

    r1 = r1.astype(BF)
    r1_here = shift(r1, "yh", 1)
    pg0 = lax.dynamic_update_slice(pair(e0, texts), pair_own(e0[:128], texts[:128]), (0, 0))
    r0 = project(jnp.dot(pg0, texts, preferred_element_type=F32), e0, n0)
    gw = (back_t(i0, r0.astype(BF)) + back_t(i1, r1)).astype(BF)
    keep, send = spread(pos, gw)
    send = shift(send, "c", 1)
    gt_send = (back_t(pg0[:, 1024:], e0) + back_t(pg1[:, 1024:], e1)).astype(BF)
    keep, send, gt_send = join(keep, send, gt_send)

    s, pg0, pg1 = join(keep.astype(F32) + send.astype(F32), pg0, pg1)
    s = near_sum(s, "x", 160)
    gt = back_t(pg0[:, :1024], e0) + back_t(pg1[:, :1024], e1)
    gt = gt + shift(gt_send, "c", 1).astype(F32)
    gt = ring_first([rows_of(gt, k, 256) for k in range(4)], "z")
    s, gt, r1_here, r0 = join(s, gt, r1_here, r0)

    s = (s[:80] + shift(s[80:].astype(BF), "yh", 1).astype(F32)).astype(BF)
    s = (s.astype(F32) + shift(s, "yl", 1).astype(F32)).astype(BF)
    gt = ring_second(*gt, "z")
    r0 = r0 + r1_here.astype(F32)
    im = ring_first([rows_of(r0, k) for k in range(4)], "x")
    raw_grad = ring_second(*im, "x").astype(BF)
    gt, gt_y, s, raw_grad = join(gt[:128], gt[128:].astype(BF), s, raw_grad)

    text_grad = gt + shift(gt_y, "yl", 1).astype(F32)
    text_unit, text_norm = unit_rows(text_feats.astype(F32))
    grad_text = unit_backward(text_grad, text_unit, text_norm)
    zp, zm, zf = shift(s, "z", 1), shift(s, "z", -1), shift(s, "z", 2)
    s = ((s.astype(F32) + zf.astype(F32)) + (zp.astype(F32) + zm.astype(F32))).astype(BF)
    o = shift(s, "c", 1)
    lo = jnp.where(core == 0, s, o)
    hi = jnp.where(core == 0, o, s)
    grad_weight = jnp.concatenate([lo, hi[16:]], 0).astype(F32)
    grad_pooled = lax.dot_general(raw_grad, weight, (((1,), (1,)), ((), ())), preferred_element_type=F32).astype(BF)
    return (grad_text, grad_pooled, grad_weight)


def solution(mesh):
    placed = (P(AXES, None), P(AXES, None), P("fsdp", None), P(), P())
    return jax.shard_map(
        local,
        mesh=mesh,
        in_specs=placed,
        out_specs=(P(AXES, None), P(AXES, None), P("fsdp", None)),
        check_vma=False,
    )
```

```python
import functools

import jax
import jax.numpy as jnp
from jax import lax
from jax.experimental import pallas as pl
from jax.experimental.pallas import tpu as pltpu
from jax.sharding import PartitionSpec as P

epsilon = 1e-06
BF = jnp.bfloat16
F32 = jnp.float32
AXES = ("dp", "fsdp")
SIZES = {"z": 4, "yl": 2, "c": 2, "x": 4, "yh": 2}


def place_of(i):
    dp, fs = divmod(i, 8)
    return {"z": dp // 4, "yl": dp // 2 % 2, "c": dp % 2, "x": fs // 2, "yh": fs % 2}


def index_of(p):
    return (p["z"] * 4 + p["yl"] * 2 + p["c"]) * 8 + p["x"] * 2 + p["yh"]


def shift(value, axis, by):
    pairs = []
    for i in range(128):
        p = place_of(i)
        p[axis] = (p[axis] + by) % SIZES[axis]
        pairs.append((i, index_of(p)))
    return lax.ppermute(value, AXES, pairs)


def join(*values):
    return lax.optimization_barrier(values)


def both_ways(block, axis):
    return shift(block, axis, -1), shift(block, axis, 1)


def rows_of(v, k, n=128):
    return v[k * n:(k + 1) * n]


def ring_first(v, axis):
    half = v[0].shape[0] // 2
    far = v[2].astype(BF)
    a = shift(far[:half], axis, 1).astype(F32)
    b = shift(far[half:], axis, -1).astype(F32)
    plus = jnp.concatenate([v[1][:half] + a, v[1][half:]], 0).astype(BF)
    minus = jnp.concatenate([v[3][:half], v[3][half:] + b], 0).astype(BF)
    return v[0], plus, minus


def ring_second(own, plus, minus, axis):
    return own + (shift(plus, axis, 1).astype(F32) + shift(minus, axis, -1).astype(F32))


def near_sum(v, axis, n=128):
    r1 = shift(rows_of(v, 1, n), axis, 1).astype(F32)
    r2 = shift(rows_of(v, 2, n), axis, 2).astype(F32)
    r3 = shift(rows_of(v, 3, n), axis, -1).astype(F32)
    return (rows_of(v, 0, n).astype(F32) + r2) + (r1 + r3)


def unit_rows(values):
    norms = jnp.sqrt(jnp.sum(values * values, axis=-1, keepdims=True) + epsilon)
    return (values / norms, norms)


def unit_backward(upstream, unit, norms):
    return (upstream - unit * jnp.sum(unit * upstream, axis=-1, keepdims=True)) / norms


def block_row(pos, dx, dy):
    x, yh = pos[0], pos[1]
    return (lax.rem(x + dx, 4) * 2 + lax.rem(yh + dy, 2)) * 144


def prepare_kernel(pos, weight, pooled, text, own, emb):
    own[pl.ds(0, 80), :] = weight[pl.ds(pl.multiple_of(pos[2] * 64, 16), 80), :]
    own[pl.ds(80, 128), :] = pooled[...]
    values = text[...].astype(F32)
    emb[...] = (values / jnp.sqrt(jnp.sum(values * values, axis=-1, keepdims=True) + epsilon)).astype(BF)


def prepare(pos, weight, pooled, text):
    return pl.pallas_call(
        prepare_kernel,
        out_shape=[jax.ShapeDtypeStruct((208, 1152), BF), jax.ShapeDtypeStruct((128, 1152), BF)],
        in_specs=[pl.BlockSpec(memory_space=pltpu.SMEM)] + [pl.BlockSpec(memory_space=pltpu.VMEM)] * 3,
        out_specs=[pl.BlockSpec(memory_space=pltpu.VMEM)] * 2,
        compiler_params=pltpu.CompilerParams(vmem_limit_bytes=32 * 2**20),
    )(pos, weight, pooled, text)


def assemble_kernel(pos, near, far, near_c, far_c, out):
    c = pos[2]
    for dx in range(4):
        for dy in range(2):
            own, oth, k = (far, far_c, 96 * dy) if dx == 2 else (near, near_c, ((0, 1, 2, 2)[dx] * 2 + dy) * 80)
            base = block_row(pos, dx, dy)
            out[pl.ds(pl.multiple_of(base + c * 64, 16), 80), :] = own[pl.ds(k, 80), :]
            out[pl.ds(pl.multiple_of(base + 80 * (1 - c), 16), 64), :] = oth[pl.ds(pl.multiple_of(k + 16 * (1 - c), 16), 64), :]


def assemble(pos, *parts):
    return pl.pallas_call(
        assemble_kernel,
        out_shape=jax.ShapeDtypeStruct((1152, 1152), BF),
        in_specs=[pl.BlockSpec(memory_space=pltpu.SMEM)] + [pl.BlockSpec(memory_space=pltpu.VMEM)] * 4,
        out_specs=pl.BlockSpec(memory_space=pltpu.VMEM),
        compiler_params=pltpu.CompilerParams(vmem_limit_bytes=32 * 2**20),
    )(pos, *parts)


def spread_kernel(pos, whole, keep, send):
    c = pos[2]
    for dx in range(4):
        for dy in range(2):
            k = dx * 2 + dy
            base = block_row(pos, dx, dy)
            keep[pl.ds(k * 80, 80), :] = whole[pl.ds(pl.multiple_of(base + c * 64, 16), 80), :]
            send[pl.ds(k * 80, 80), :] = whole[pl.ds(pl.multiple_of(base + (1 - c) * 64, 16), 80), :]


def spread(pos, whole):
    return pl.pallas_call(
        spread_kernel,
        out_shape=[jax.ShapeDtypeStruct((640, 1152), BF)] * 2,
        in_specs=[pl.BlockSpec(memory_space=pltpu.SMEM), pl.BlockSpec(memory_space=pltpu.VMEM)],
        out_specs=[pl.BlockSpec(memory_space=pltpu.VMEM)] * 2,
        compiler_params=pltpu.CompilerParams(vmem_limit_bytes=32 * 2**20),
    )(pos, whole)


def local(pooled, text_feats, out_weight, logit_scale, logit_bias):
    dp = lax.axis_index("dp")
    fs = lax.axis_index("fsdp")
    core = dp % 2
    pos = jnp.stack([fs // 2, fs % 2, core]).astype(jnp.int32)
    mult = logit_scale[0]
    bias = logit_bias[0]

    own, text_emb = prepare(pos, out_weight, pooled, text_feats)
    oth = shift(own, "yh", 1)
    own_p, own_m = both_ways(own, "x")
    oth_p, oth_m = both_ways(oth, "x")
    far_a = shift(jnp.concatenate([own_m[:96], oth_m[:96]], 0), "x", 1)
    far_b = shift(jnp.concatenate([own_p[96:], oth_p[96:]], 0), "x", -1)
    w_near = jnp.concatenate([v[:80] for v in (own, oth, own_p, oth_p, own_m, oth_m)], 0)
    w_far_c = shift(far_a, "c", 1)
    weight = assemble(pos, w_near, far_a, shift(w_near, "c", 1), w_far_c)
    images = jnp.concatenate([
        pooled, own_p[80:], far_a[80:96], far_b[:112], own_m[80:],
        oth[80:], oth_p[80:], far_a[176:], far_b[112:], oth_m[80:]], 0)

    text_own, _ = join(text_emb, oth)
    text_oth = shift(text_own, "yl", 1)
    t_p, t_m = both_ways(text_emb, "z")
    u_p, u_m = both_ways(text_oth, "z")
    fa = shift(jnp.concatenate([t_m[:64], u_m[:64]], 0), "z", 1)
    fb = shift(jnp.concatenate([t_p[64:], u_p[64:]], 0), "z", -1)
    t_near = jnp.concatenate([text_emb, text_oth, t_p, u_p, t_m, u_m], 0)
    t_far = jnp.concatenate([fa[:64], fb[:64], fa[64:], fb[64:]], 0)
    t_near, t_far, _ = join(t_near, t_far, w_far_c)
    c_near = shift(t_near, "c", 1)
    c_far = shift(t_far, "c", 1)
    texts = jnp.concatenate([t_near[:512], t_far, t_near[512:], c_near[:512], c_far, c_near[512:]], 0)

    def embed(rows):
        raw = jnp.dot(rows, weight, preferred_element_type=F32)
        unit, norm = unit_rows(raw)
        return unit.astype(BF), norm

    emb, norm = embed(images)

    def pair(e, t):
        logits = mult * lax.dot_general(e, t, (((1,), (1,)), ((), ())), preferred_element_type=F32) + bias
        return (jax.nn.sigmoid(logits) * mult).astype(BF)

    def pair_own(e, t):
        logits = mult * lax.dot_general(e, t, (((1,), (1,)), ((), ())), preferred_element_type=F32) + bias
        row = lax.broadcasted_iota(jnp.int32, logits.shape, 0)
        col = lax.broadcasted_iota(jnp.int32, logits.shape, 1)
        sign = jnp.where(row == col, 1.0, -1.0)
        return (-sign * jax.nn.sigmoid(-sign * logits) * mult).astype(BF)

    def back_t(pg, e):
        return lax.dot_general(pg, e, (((0,), (0,)), ((), ())), preferred_element_type=F32)

    def project(g, e, n):
        return unit_backward(g, e.astype(F32), n)

    grads = lax.dynamic_update_slice(pair(emb, texts), pair_own(emb[:128], texts[:128]), (0, 0))
    raw = project(jnp.dot(grads, texts, preferred_element_type=F32), emb, norm).astype(BF)
    r0 = raw[:512]

    r1_here = shift(raw[512:], "yh", 1)
    gw = back_t(images, raw).astype(BF)
    keep, send = spread(pos, gw)
    send = shift(send, "c", 1)
    gt_send = back_t(grads[:, 1024:], emb)
    keep, send, gt_send = join(keep, send, gt_send)
    gt_send = gt_send.astype(BF)

    s, grads = join((keep.astype(F32) + send.astype(F32)).astype(BF), grads)
    s = near_sum(s, "x", 160)
    gt = back_t(grads[:, :1024], emb)
    gt = gt + shift(gt_send, "c", 1).astype(F32)
    gt = ring_first([rows_of(gt, k, 256) for k in range(4)], "z")
    s, gt, r0 = join(s, gt, r0)

    s = (s[:80] + shift(s[80:].astype(BF), "yh", 1).astype(F32)).astype(BF)
    s = (s.astype(F32) + shift(s, "yl", 1).astype(F32)).astype(BF)
    gt = ring_second(*gt, "z")
    r0 = r0.astype(F32) + r1_here.astype(F32)
    raw_grad = near_sum(r0.astype(BF), "x").astype(BF)
    gt, gt_y, s, raw_grad = join(gt[:128], gt[128:].astype(BF), s, raw_grad)

    text_grad = gt + shift(gt_y, "yl", 1).astype(F32)
    text_unit, text_norm = unit_rows(text_feats.astype(F32))
    grad_text = unit_backward(text_grad, text_unit, text_norm)
    zp, zm, zf = shift(s, "z", 1), shift(s, "z", -1), shift(s, "z", 2)
    s = ((s.astype(F32) + zf.astype(F32)) + (zp.astype(F32) + zm.astype(F32))).astype(BF)
    o = shift(s, "c", 1)
    lo = jnp.where(core == 0, s, o)
    hi = jnp.where(core == 0, o, s)
    grad_weight = jnp.concatenate([lo, hi[16:]], 0).astype(F32)
    grad_pooled = lax.dot_general(raw_grad, weight, (((1,), (1,)), ((), ())), preferred_element_type=F32).astype(BF)
    return (grad_text, grad_pooled, grad_weight)


def solution(mesh):
    placed = (P(AXES, None), P(AXES, None), P("fsdp", None), P(), P())
    return jax.shard_map(
        local,
        mesh=mesh,
        in_specs=placed,
        out_specs=(P(AXES, None), P(AXES, None), P("fsdp", None)),
        check_vma=False,
    )
```

```python
import functools

import jax
import jax.numpy as jnp
from jax import lax
from jax.experimental import pallas as pl
from jax.experimental.pallas import tpu as pltpu
from jax.sharding import PartitionSpec as P

epsilon = 1e-06
BF = jnp.bfloat16
F32 = jnp.float32
AXES = ("dp", "fsdp")
SIZES = {"z": 4, "yl": 2, "c": 2, "x": 4, "yh": 2}


def place_of(i):
    dp, fs = divmod(i, 8)
    return {"z": dp // 4, "yl": dp // 2 % 2, "c": dp % 2, "x": fs // 2, "yh": fs % 2}


def index_of(p):
    return (p["z"] * 4 + p["yl"] * 2 + p["c"]) * 8 + p["x"] * 2 + p["yh"]


def shift(value, axis, by):
    pairs = []
    for i in range(128):
        p = place_of(i)
        p[axis] = (p[axis] + by) % SIZES[axis]
        pairs.append((i, index_of(p)))
    return lax.ppermute(value, AXES, pairs)


def join(*values):
    return lax.optimization_barrier(values)


def both_ways(block, axis):
    return shift(block, axis, -1), shift(block, axis, 1)


def rows_of(v, k, n=128):
    return v[k * n:(k + 1) * n]


def ring_first(v, axis):
    half = v[0].shape[0] // 2
    far = v[2].astype(BF)
    a = shift(far[:half], axis, 1).astype(F32)
    b = shift(far[half:], axis, -1).astype(F32)
    plus = jnp.concatenate([v[1][:half] + a, v[1][half:]], 0).astype(BF)
    minus = jnp.concatenate([v[3][:half], v[3][half:] + b], 0).astype(BF)
    return v[0], plus, minus


def ring_second(own, plus, minus, axis):
    return own + (shift(plus, axis, 1).astype(F32) + shift(minus, axis, -1).astype(F32))


def near_sum(v, axis, n=128):
    r1 = shift(rows_of(v, 1, n), axis, 1).astype(F32)
    r2 = shift(rows_of(v, 2, n), axis, 2).astype(F32)
    r3 = shift(rows_of(v, 3, n), axis, -1).astype(F32)
    return (rows_of(v, 0, n).astype(F32) + r2) + (r1 + r3)


def unit_rows(values):
    norms = jnp.sqrt(jnp.sum(values * values, axis=-1, keepdims=True) + epsilon)
    return (values / norms, norms)


def unit_backward(upstream, unit, norms):
    return (upstream - unit * jnp.sum(unit * upstream, axis=-1, keepdims=True)) / norms


def block_row(pos, dx, dy):
    x, yh = pos[0], pos[1]
    return (lax.rem(x + dx, 4) * 2 + lax.rem(yh + dy, 2)) * 144


def prepare_kernel(pos, weight, pooled, text, own, emb):
    own[pl.ds(0, 80), :] = weight[pl.ds(pl.multiple_of(pos[2] * 64, 16), 80), :]
    own[pl.ds(80, 128), :] = pooled[...]
    values = text[...].astype(F32)
    emb[...] = (values / jnp.sqrt(jnp.sum(values * values, axis=-1, keepdims=True) + epsilon)).astype(BF)


def prepare(pos, weight, pooled, text):
    return pl.pallas_call(
        prepare_kernel,
        out_shape=[jax.ShapeDtypeStruct((208, 1152), BF), jax.ShapeDtypeStruct((128, 1152), BF)],
        in_specs=[pl.BlockSpec(memory_space=pltpu.SMEM)] + [pl.BlockSpec(memory_space=pltpu.VMEM)] * 3,
        out_specs=[pl.BlockSpec(memory_space=pltpu.VMEM)] * 2,
        compiler_params=pltpu.CompilerParams(vmem_limit_bytes=32 * 2**20),
    )(pos, weight, pooled, text)


def assemble_kernel(pos, near, far, near_c, far_c, out):
    c = pos[2]
    for dx in range(4):
        for dy in range(2):
            own, oth, k = (far, far_c, 96 * dy) if dx == 2 else (near, near_c, ((0, 1, 2, 2)[dx] * 2 + dy) * 80)
            base = block_row(pos, dx, dy)
            out[pl.ds(pl.multiple_of(base + c * 64, 16), 80), :] = own[pl.ds(k, 80), :]
            out[pl.ds(pl.multiple_of(base + 80 * (1 - c), 16), 64), :] = oth[pl.ds(pl.multiple_of(k + 16 * (1 - c), 16), 64), :]


def assemble(pos, *parts):
    return pl.pallas_call(
        assemble_kernel,
        out_shape=jax.ShapeDtypeStruct((1152, 1152), BF),
        in_specs=[pl.BlockSpec(memory_space=pltpu.SMEM)] + [pl.BlockSpec(memory_space=pltpu.VMEM)] * 4,
        out_specs=pl.BlockSpec(memory_space=pltpu.VMEM),
        compiler_params=pltpu.CompilerParams(vmem_limit_bytes=32 * 2**20),
    )(pos, *parts)


def spread_kernel(pos, whole, keep, send):
    c = pos[2]
    for dx in range(4):
        for dy in range(2):
            k = dx * 2 + dy
            base = block_row(pos, dx, dy)
            keep[pl.ds(k * 80, 80), :] = whole[pl.ds(pl.multiple_of(base + c * 64, 16), 80), :]
            send[pl.ds(k * 80, 80), :] = whole[pl.ds(pl.multiple_of(base + (1 - c) * 64, 16), 80), :]


def spread(pos, whole):
    return pl.pallas_call(
        spread_kernel,
        out_shape=[jax.ShapeDtypeStruct((640, 1152), BF)] * 2,
        in_specs=[pl.BlockSpec(memory_space=pltpu.SMEM), pl.BlockSpec(memory_space=pltpu.VMEM)],
        out_specs=[pl.BlockSpec(memory_space=pltpu.VMEM)] * 2,
        compiler_params=pltpu.CompilerParams(vmem_limit_bytes=32 * 2**20),
    )(pos, whole)


def local(pooled, text_feats, out_weight, logit_scale, logit_bias):
    dp = lax.axis_index("dp")
    fs = lax.axis_index("fsdp")
    core = dp % 2
    pos = jnp.stack([fs // 2, fs % 2, core]).astype(jnp.int32)
    mult = logit_scale[0]
    bias = logit_bias[0]

    own, text_emb = prepare(pos, out_weight, pooled, text_feats)
    oth = shift(own, "yh", 1)
    own_p, own_m = both_ways(own, "x")
    oth_p, oth_m = both_ways(oth, "x")
    far_a = shift(jnp.concatenate([own_m[:96], oth_m[:96]], 0), "x", 1)
    far_b = shift(jnp.concatenate([own_p[96:], oth_p[96:]], 0), "x", -1)
    w_near = jnp.concatenate([v[:80] for v in (own, oth, own_p, oth_p, own_m, oth_m)], 0)
    w_far_c = shift(far_a, "c", 1)
    weight = assemble(pos, w_near, far_a, shift(w_near, "c", 1), w_far_c)
    images = jnp.concatenate([
        pooled, own_p[80:], far_a[80:96], far_b[:112], own_m[80:],
        oth[80:], oth_p[80:], far_a[176:], far_b[112:], oth_m[80:]], 0)

    text_own, _ = join(text_emb, oth)
    text_oth = shift(text_own, "yl", 1)
    t_p, t_m = both_ways(text_emb, "z")
    u_p, u_m = both_ways(text_oth, "z")
    fa = shift(jnp.concatenate([t_m[:64], u_m[:64]], 0), "z", 1)
    fb = shift(jnp.concatenate([t_p[64:], u_p[64:]], 0), "z", -1)
    t_near = jnp.concatenate([text_emb, text_oth, t_p, u_p, t_m, u_m], 0)
    t_far = jnp.concatenate([fa[:64], fb[:64], fa[64:], fb[64:]], 0)
    t_near, t_far, _ = join(t_near, t_far, w_far_c)
    c_near = shift(t_near, "c", 1)
    c_far = shift(t_far, "c", 1)
    texts = jnp.concatenate([t_near[:512], t_far, t_near[512:], c_near[:512], c_far, c_near[512:]], 0)

    def embed(rows):
        raw = jnp.dot(rows, weight, preferred_element_type=F32)
        unit, norm = unit_rows(raw)
        return unit.astype(BF), norm

    emb, norm = embed(images)

    def pair(e, t):
        logits = mult * lax.dot_general(e, t, (((1,), (1,)), ((), ())), preferred_element_type=F32) + bias
        return (jax.nn.sigmoid(logits) * mult).astype(BF)

    def pair_own(e, t):
        logits = mult * lax.dot_general(e, t, (((1,), (1,)), ((), ())), preferred_element_type=F32) + bias
        row = lax.broadcasted_iota(jnp.int32, logits.shape, 0)
        col = lax.broadcasted_iota(jnp.int32, logits.shape, 1)
        sign = jnp.where(row == col, 1.0, -1.0)
        return (-sign * jax.nn.sigmoid(-sign * logits) * mult).astype(BF)

    def back_t(pg, e):
        return lax.dot_general(pg, e, (((0,), (0,)), ((), ())), preferred_element_type=F32)

    def project(g, e, n):
        return unit_backward(g, e.astype(F32), n)

    grads = lax.dynamic_update_slice(pair(emb, texts), pair_own(emb[:128], texts[:128]), (0, 0))
    r0 = project(jnp.dot(grads[:512], texts, preferred_element_type=F32), emb[:512], norm[:512]).astype(BF)
    r1 = project(jnp.dot(grads[512:], texts, preferred_element_type=F32), emb[512:], norm[512:]).astype(BF)

    r1_here = shift(r1, "yh", 1)
    gw = (back_t(images[:512], r0) + back_t(images[512:], r1)).astype(BF)
    keep, send = spread(pos, gw)
    send = shift(send, "c", 1)
    gt_send = back_t(grads[:, 1024:], emb)
    keep, send, gt_send = join(keep, send, gt_send)
    gt_send = gt_send.astype(BF)

    s, grads = join((keep.astype(F32) + send.astype(F32)).astype(BF), grads)
    s = near_sum(s, "x", 160)
    gt = back_t(grads[:, :1024], emb)
    gt = gt + shift(gt_send, "c", 1).astype(F32)
    gt = ring_first([rows_of(gt, k, 256) for k in range(4)], "z")
    s, gt, r0 = join(s, gt, r0)

    s = (s[:80] + shift(s[80:].astype(BF), "yh", 1).astype(F32)).astype(BF)
    s = (s.astype(F32) + shift(s, "yl", 1).astype(F32)).astype(BF)
    gt = ring_second(*gt, "z")
    r0 = r0.astype(F32) + r1_here.astype(F32)
    raw_grad = near_sum(r0.astype(BF), "x").astype(BF)
    gt, gt_y, s, raw_grad = join(gt[:128], gt[128:].astype(BF), s, raw_grad)

    text_grad = gt + shift(gt_y, "yl", 1).astype(F32)
    text_unit, text_norm = unit_rows(text_feats.astype(F32))
    grad_text = unit_backward(text_grad, text_unit, text_norm)
    zp, zm, zf = shift(s, "z", 1), shift(s, "z", -1), shift(s, "z", 2)
    s = ((s.astype(F32) + zf.astype(F32)) + (zp.astype(F32) + zm.astype(F32))).astype(BF)
    o = shift(s, "c", 1)
    lo = jnp.where(core == 0, s, o)
    hi = jnp.where(core == 0, o, s)
    grad_weight = jnp.concatenate([lo, hi[16:]], 0).astype(F32)
    grad_pooled = lax.dot_general(raw_grad, weight, (((1,), (1,)), ((), ())), preferred_element_type=F32).astype(BF)
    return (grad_text, grad_pooled, grad_weight)


def solution(mesh):
    placed = (P(AXES, None), P(AXES, None), P("fsdp", None), P(), P())
    return jax.shard_map(
        local,
        mesh=mesh,
        in_specs=placed,
        out_specs=(P(AXES, None), P(AXES, None), P("fsdp", None)),
        check_vma=False,
    )
```

```python
import functools

import jax
import jax.numpy as jnp
from jax import lax
from jax.experimental import pallas as pl
from jax.experimental.pallas import tpu as pltpu
from jax.sharding import PartitionSpec as P

epsilon = 1e-06
BF = jnp.bfloat16
F32 = jnp.float32
AXES = ("dp", "fsdp")
SIZES = {"z": 4, "yl": 2, "c": 2, "x": 4, "yh": 2}


def place_of(i):
    dp, fs = divmod(i, 8)
    return {"z": dp // 4, "yl": dp // 2 % 2, "c": dp % 2, "x": fs // 2, "yh": fs % 2}


def index_of(p):
    return (p["z"] * 4 + p["yl"] * 2 + p["c"]) * 8 + p["x"] * 2 + p["yh"]


def shift(value, axis, by):
    pairs = []
    for i in range(128):
        p = place_of(i)
        p[axis] = (p[axis] + by) % SIZES[axis]
        pairs.append((i, index_of(p)))
    return lax.ppermute(value, AXES, pairs)


def join(*values):
    return lax.optimization_barrier(values)


def both_ways(block, axis):
    return shift(block, axis, -1), shift(block, axis, 1)


def rows_of(v, k, n=128):
    return v[k * n:(k + 1) * n]


def ring_first(v, axis):
    half = v[0].shape[0] // 2
    far = v[2].astype(BF)
    a = shift(far[:half], axis, 1).astype(F32)
    b = shift(far[half:], axis, -1).astype(F32)
    plus = jnp.concatenate([v[1][:half] + a, v[1][half:]], 0).astype(BF)
    minus = jnp.concatenate([v[3][:half], v[3][half:] + b], 0).astype(BF)
    return v[0], plus, minus


def ring_second(own, plus, minus, axis):
    return own + (shift(plus, axis, 1).astype(F32) + shift(minus, axis, -1).astype(F32))


def near_sum(v, axis, n=128):
    r1 = shift(rows_of(v, 1, n), axis, 1).astype(F32)
    r2 = shift(rows_of(v, 2, n), axis, 2).astype(F32)
    r3 = shift(rows_of(v, 3, n), axis, -1).astype(F32)
    return (rows_of(v, 0, n).astype(F32) + r2) + (r1 + r3)


def unit_rows(values):
    norms = jnp.sqrt(jnp.sum(values * values, axis=-1, keepdims=True) + epsilon)
    return (values / norms, norms)


def unit_backward(upstream, unit, norms):
    return (upstream - unit * jnp.sum(unit * upstream, axis=-1, keepdims=True)) / norms


def block_row(pos, dx, dy):
    x, yh = pos[0], pos[1]
    return (lax.rem(x + dx, 4) * 2 + lax.rem(yh + dy, 2)) * 144


def prepare_kernel(pos, weight, pooled, text, own, emb):
    own[pl.ds(0, 80), :] = weight[pl.ds(pl.multiple_of(pos[2] * 64, 16), 80), :]
    own[pl.ds(80, 128), :] = pooled[...]
    values = text[...].astype(F32)
    emb[...] = (values / jnp.sqrt(jnp.sum(values * values, axis=-1, keepdims=True) + epsilon)).astype(BF)


def prepare(pos, weight, pooled, text):
    return pl.pallas_call(
        prepare_kernel,
        out_shape=[jax.ShapeDtypeStruct((208, 1152), BF), jax.ShapeDtypeStruct((128, 1152), BF)],
        in_specs=[pl.BlockSpec(memory_space=pltpu.SMEM)] + [pl.BlockSpec(memory_space=pltpu.VMEM)] * 3,
        out_specs=[pl.BlockSpec(memory_space=pltpu.VMEM)] * 2,
        compiler_params=pltpu.CompilerParams(vmem_limit_bytes=32 * 2**20),
    )(pos, weight, pooled, text)


def assemble_kernel(pos, near, far, near_c, far_c, out):
    c = pos[2]
    for dx in range(4):
        for dy in range(2):
            own, oth, k = (far, far_c, 96 * dy) if dx == 2 else (near, near_c, ((0, 1, 2, 2)[dx] * 2 + dy) * 80)
            base = block_row(pos, dx, dy)
            out[pl.ds(pl.multiple_of(base + c * 64, 16), 80), :] = own[pl.ds(k, 80), :]
            out[pl.ds(pl.multiple_of(base + 80 * (1 - c), 16), 64), :] = oth[pl.ds(pl.multiple_of(k + 16 * (1 - c), 16), 64), :]


def assemble(pos, *parts):
    return pl.pallas_call(
        assemble_kernel,
        out_shape=jax.ShapeDtypeStruct((1152, 1152), BF),
        in_specs=[pl.BlockSpec(memory_space=pltpu.SMEM)] + [pl.BlockSpec(memory_space=pltpu.VMEM)] * 4,
        out_specs=pl.BlockSpec(memory_space=pltpu.VMEM),
        compiler_params=pltpu.CompilerParams(vmem_limit_bytes=32 * 2**20),
    )(pos, *parts)


def give_kernel(pos, whole, send):
    c = pos[2]
    for dx in range(4):
        for dy in range(2):
            row = pl.multiple_of(block_row(pos, dx, dy) + (1 - c) * 64, 16)
            send[pl.ds((dx * 2 + dy) * 80, 80), :] = whole[pl.ds(row, 80), :]


def take_kernel(pos, whole, got, out):
    c = pos[2]
    for dx in range(4):
        for dy in range(2):
            row = pl.multiple_of(block_row(pos, dx, dy) + c * 64, 16)
            at = pl.ds((dx * 2 + dy) * 80, 80)
            out[at, :] = (whole[pl.ds(row, 80), :].astype(F32) + got[at, :].astype(F32)).astype(BF)


def by_blocks(kernel, pos, *arrays):
    return pl.pallas_call(
        kernel,
        out_shape=jax.ShapeDtypeStruct((640, 1152), BF),
        in_specs=[pl.BlockSpec(memory_space=pltpu.SMEM)] + [pl.BlockSpec(memory_space=pltpu.VMEM)] * len(arrays),
        out_specs=pl.BlockSpec(memory_space=pltpu.VMEM),
        compiler_params=pltpu.CompilerParams(vmem_limit_bytes=32 * 2**20),
    )(pos, *arrays)


def local(pooled, text_feats, out_weight, logit_scale, logit_bias):
    dp = lax.axis_index("dp")
    fs = lax.axis_index("fsdp")
    core = dp % 2
    pos = jnp.stack([fs // 2, fs % 2, core]).astype(jnp.int32)
    mult = logit_scale[0]
    bias = logit_bias[0]

    own, text_emb = prepare(pos, out_weight, pooled, text_feats)
    oth = shift(own, "yh", 1)
    own_p, own_m = both_ways(own, "x")
    oth_p, oth_m = both_ways(oth, "x")
    far_a = shift(jnp.concatenate([own_m[:96], oth_m[:96]], 0), "x", 1)
    far_b = shift(jnp.concatenate([own_p[96:], oth_p[96:]], 0), "x", -1)
    w_near = jnp.concatenate([v[:80] for v in (own, oth, own_p, oth_p, own_m, oth_m)], 0)
    w_far_c = shift(far_a, "c", 1)
    weight = assemble(pos, w_near, far_a, shift(w_near, "c", 1), w_far_c)
    images = jnp.concatenate([
        pooled, own_p[80:], far_a[80:96], far_b[:112], own_m[80:],
        oth[80:], oth_p[80:], far_a[176:], far_b[112:], oth_m[80:]], 0)

    text_own, _ = join(text_emb, oth)
    text_oth = shift(text_own, "yl", 1)
    t_p, t_m = both_ways(text_emb, "z")
    u_p, u_m = both_ways(text_oth, "z")
    fa = shift(jnp.concatenate([t_m[:64], u_m[:64]], 0), "z", 1)
    fb = shift(jnp.concatenate([t_p[64:], u_p[64:]], 0), "z", -1)
    t_near = jnp.concatenate([text_emb, text_oth, t_p, u_p, t_m, u_m], 0)
    t_far = jnp.concatenate([fa[:64], fb[:64], fa[64:], fb[64:]], 0)
    t_far, _ = join(t_far, w_far_c)
    c_near = shift(t_near, "c", 1)
    c_far = shift(t_far, "c", 1)
    texts = jnp.concatenate([t_near[:512], t_far, t_near[512:], c_near[:512], c_far, c_near[512:]], 0)

    def embed(rows):
        raw = jnp.dot(rows, weight, preferred_element_type=F32)
        unit, norm = unit_rows(raw)
        return unit.astype(BF), norm

    emb, norm = embed(images)

    def pair(e, t):
        logits = mult * lax.dot_general(e, t, (((1,), (1,)), ((), ())), preferred_element_type=F32) + bias
        return (jax.nn.sigmoid(logits) * mult).astype(BF)

    def pair_own(e, t):
        logits = mult * lax.dot_general(e, t, (((1,), (1,)), ((), ())), preferred_element_type=F32) + bias
        row = lax.broadcasted_iota(jnp.int32, logits.shape, 0)
        col = lax.broadcasted_iota(jnp.int32, logits.shape, 1)
        sign = jnp.where(row == col, 1.0, -1.0)
        return (-sign * jax.nn.sigmoid(-sign * logits) * mult).astype(BF)

    def back_t(pg, e):
        return lax.dot_general(pg, e, (((0,), (0,)), ((), ())), preferred_element_type=F32)

    def project(g, e, n):
        return unit_backward(g, e.astype(F32), n)

    grads = lax.dynamic_update_slice(pair(emb, texts), pair_own(emb[:128], texts[:128]), (0, 0))
    r0 = project(jnp.dot(grads[:512], texts, preferred_element_type=F32), emb[:512], norm[:512]).astype(BF)
    r1 = project(jnp.dot(grads[512:], texts, preferred_element_type=F32), emb[512:], norm[512:]).astype(BF)

    r1_here = shift(r1, "yh", 1)
    gw = (back_t(images[:512], r0) + back_t(images[512:], r1)).astype(BF)
    send = shift(by_blocks(give_kernel, pos, gw), "c", 1)
    gt_send = back_t(grads[:, 1024:], emb)
    send, gt_send = join(send, gt_send)
    gt_send = gt_send.astype(BF)

    s, grads = join(by_blocks(take_kernel, pos, gw, send), grads)
    s = near_sum(s, "x", 160)
    gt = back_t(grads[:, :1024], emb)
    gt = gt + shift(gt_send, "c", 1).astype(F32)
    gt = ring_first([rows_of(gt, k, 256) for k in range(4)], "z")
    s, gt, r0 = join(s, gt, r0)

    s = (s[:80] + shift(s[80:].astype(BF), "yh", 1).astype(F32)).astype(BF)
    s = (s.astype(F32) + shift(s, "yl", 1).astype(F32)).astype(BF)
    gt = ring_second(*gt, "z")
    r0 = r0.astype(F32) + r1_here.astype(F32)
    raw_grad = near_sum(r0.astype(BF), "x").astype(BF)
    gt, gt_y, s, raw_grad = join(gt[:128], gt[128:].astype(BF), s, raw_grad)

    text_grad = gt + shift(gt_y, "yl", 1).astype(F32)
    text_unit, text_norm = unit_rows(text_feats.astype(F32))
    grad_text = unit_backward(text_grad, text_unit, text_norm)
    zp, zm, zf = shift(s, "z", 1), shift(s, "z", -1), shift(s, "z", 2)
    s = ((s.astype(F32) + zf.astype(F32)) + (zp.astype(F32) + zm.astype(F32))).astype(BF)
    o = shift(s, "c", 1)
    lo = jnp.where(core == 0, s, o)
    hi = jnp.where(core == 0, o, s)
    grad_weight = jnp.concatenate([lo, hi[16:]], 0).astype(F32)
    grad_pooled = lax.dot_general(raw_grad, weight, (((1,), (1,)), ((), ())), preferred_element_type=F32).astype(BF)
    return (grad_text, grad_pooled, grad_weight)


def solution(mesh):
    placed = (P(AXES, None), P(AXES, None), P("fsdp", None), P(), P())
    return jax.shard_map(
        local,
        mesh=mesh,
        in_specs=placed,
        out_specs=(P(AXES, None), P(AXES, None), P("fsdp", None)),
        check_vma=False,
    )
```

```python
import functools

import jax
import jax.numpy as jnp
from jax import lax
from jax.experimental import pallas as pl
from jax.experimental.pallas import tpu as pltpu
from jax.sharding import PartitionSpec as P

epsilon = 1e-06
BF = jnp.bfloat16
F32 = jnp.float32
AXES = ("dp", "fsdp")
SIZES = {"z": 4, "yl": 2, "c": 2, "x": 4, "yh": 2}


def place_of(i):
    dp, fs = divmod(i, 8)
    return {"z": dp // 4, "yl": dp // 2 % 2, "c": dp % 2, "x": fs // 2, "yh": fs % 2}


def index_of(p):
    return (p["z"] * 4 + p["yl"] * 2 + p["c"]) * 8 + p["x"] * 2 + p["yh"]


def shift(value, axis, by):
    pairs = []
    for i in range(128):
        p = place_of(i)
        p[axis] = (p[axis] + by) % SIZES[axis]
        pairs.append((i, index_of(p)))
    return lax.ppermute(value, AXES, pairs)


def join(*values):
    return lax.optimization_barrier(values)


def both_ways(block, axis):
    return shift(block, axis, -1), shift(block, axis, 1)


def rows_of(v, k, n=128):
    return v[k * n:(k + 1) * n]


def ring_first(v, axis):
    half = v[0].shape[0] // 2
    far = v[2].astype(BF)
    a = shift(far[:half], axis, 1).astype(F32)
    b = shift(far[half:], axis, -1).astype(F32)
    plus = jnp.concatenate([v[1][:half] + a, v[1][half:]], 0).astype(BF)
    minus = jnp.concatenate([v[3][:half], v[3][half:] + b], 0).astype(BF)
    return v[0], plus, minus


def ring_second(own, plus, minus, axis):
    return own + (shift(plus, axis, 1).astype(F32) + shift(minus, axis, -1).astype(F32))


def near_sum(v, axis, n=128):
    r1 = shift(rows_of(v, 1, n), axis, 1).astype(F32)
    r2 = shift(rows_of(v, 2, n), axis, 2).astype(F32)
    r3 = shift(rows_of(v, 3, n), axis, -1).astype(F32)
    return (rows_of(v, 0, n).astype(F32) + r2) + (r1 + r3)


def unit_rows(values):
    norms = jnp.sqrt(jnp.sum(values * values, axis=-1, keepdims=True) + epsilon)
    return (values / norms, norms)


def unit_backward(upstream, unit, norms):
    return (upstream - unit * jnp.sum(unit * upstream, axis=-1, keepdims=True)) / norms


def block_row(pos, dx, dy):
    x, yh = pos[0], pos[1]
    return (lax.rem(x + dx, 4) * 2 + lax.rem(yh + dy, 2)) * 144


def prepare_kernel(weight, pooled, text, own, emb, held, sems):
    core = lax.rem(lax.axis_index("dp"), 2)
    share = weight.at[pl.ds(pl.multiple_of(core * 64, 16), 80)]
    copies = [
        pltpu.make_async_copy(text, held, sems.at[0]),
        pltpu.make_async_copy(share, own.at[pl.ds(0, 80)], sems.at[1]),
        pltpu.make_async_copy(pooled, own.at[pl.ds(80, 128)], sems.at[2]),
    ]
    for copy in copies:
        copy.start()
    for copy in copies:
        copy.wait()
    values = held[...].astype(F32)
    emb[...] = (values / jnp.sqrt(jnp.sum(values * values, axis=-1, keepdims=True) + epsilon)).astype(BF)


def prepare(weight, pooled, text):
    return pl.pallas_call(
        prepare_kernel,
        out_shape=[jax.ShapeDtypeStruct((208, 1152), BF), jax.ShapeDtypeStruct((128, 1152), BF)],
        in_specs=[pl.BlockSpec(memory_space=pl.ANY)] * 3,
        out_specs=[pl.BlockSpec(memory_space=pltpu.VMEM)] * 2,
        scratch_shapes=[pltpu.VMEM((128, 1152), BF), pltpu.SemaphoreType.DMA((3,))],
        compiler_params=pltpu.CompilerParams(vmem_limit_bytes=63 * 2**20),
    )(weight, pooled, text)


def assemble_kernel(pos, near, far, near_c, far_c, out):
    c = pos[2]
    for dx in range(4):
        for dy in range(2):
            own, oth, k = (far, far_c, 96 * dy) if dx == 2 else (near, near_c, ((0, 1, 2, 2)[dx] * 2 + dy) * 80)
            base = block_row(pos, dx, dy)
            out[pl.ds(pl.multiple_of(base + c * 64, 16), 80), :] = own[pl.ds(k, 80), :]
            out[pl.ds(pl.multiple_of(base + 80 * (1 - c), 16), 64), :] = oth[pl.ds(pl.multiple_of(k + 16 * (1 - c), 16), 64), :]


def assemble(pos, *parts):
    return pl.pallas_call(
        assemble_kernel,
        out_shape=jax.ShapeDtypeStruct((1152, 1152), BF),
        in_specs=[pl.BlockSpec(memory_space=pltpu.SMEM)] + [pl.BlockSpec(memory_space=pltpu.VMEM)] * 4,
        out_specs=pl.BlockSpec(memory_space=pltpu.VMEM),
        compiler_params=pltpu.CompilerParams(vmem_limit_bytes=32 * 2**20),
    )(pos, *parts)


def spread_kernel(pos, whole, keep, send):
    c = pos[2]
    for dx in range(4):
        for dy in range(2):
            k = dx * 2 + dy
            base = block_row(pos, dx, dy)
            keep[pl.ds(k * 80, 80), :] = whole[pl.ds(pl.multiple_of(base + c * 64, 16), 80), :]
            send[pl.ds(k * 80, 80), :] = whole[pl.ds(pl.multiple_of(base + (1 - c) * 64, 16), 80), :]


def spread(pos, whole):
    return pl.pallas_call(
        spread_kernel,
        out_shape=[jax.ShapeDtypeStruct((640, 1152), BF)] * 2,
        in_specs=[pl.BlockSpec(memory_space=pltpu.SMEM), pl.BlockSpec(memory_space=pltpu.VMEM)],
        out_specs=[pl.BlockSpec(memory_space=pltpu.VMEM)] * 2,
        compiler_params=pltpu.CompilerParams(vmem_limit_bytes=32 * 2**20),
    )(pos, whole)


def local(pooled, text_feats, out_weight, logit_scale, logit_bias):
    dp = lax.axis_index("dp")
    fs = lax.axis_index("fsdp")
    core = dp % 2
    pos = jnp.stack([fs // 2, fs % 2, core]).astype(jnp.int32)
    mult = logit_scale[0]
    bias = logit_bias[0]

    own, text_emb = prepare(out_weight, pooled, text_feats)
    oth = shift(own, "yh", 1)
    own_p, own_m = both_ways(own, "x")
    oth_p, oth_m = both_ways(oth, "x")
    far_a = shift(jnp.concatenate([own_m[:96], oth_m[:96]], 0), "x", 1)
    far_b = shift(jnp.concatenate([own_p[96:], oth_p[96:]], 0), "x", -1)
    w_near = jnp.concatenate([v[:80] for v in (own, oth, own_p, oth_p, own_m, oth_m)], 0)
    w_far_c = shift(far_a, "c", 1)
    weight = assemble(pos, w_near, far_a, shift(w_near, "c", 1), w_far_c)
    images = jnp.concatenate([
        pooled, own_p[80:], far_a[80:96], far_b[:112], own_m[80:],
        oth[80:], oth_p[80:], far_a[176:], far_b[112:], oth_m[80:]], 0)

    text_own, _ = join(text_emb, oth)
    text_oth = shift(text_own, "yl", 1)
    t_p, t_m = both_ways(text_emb, "z")
    u_p, u_m = both_ways(text_oth, "z")
    fa = shift(jnp.concatenate([t_m[:64], u_m[:64]], 0), "z", 1)
    fb = shift(jnp.concatenate([t_p[64:], u_p[64:]], 0), "z", -1)
    t_near = jnp.concatenate([text_emb, text_oth, t_p, u_p, t_m, u_m], 0)
    t_far = jnp.concatenate([fa[:64], fb[:64], fa[64:], fb[64:]], 0)
    t_near, t_far, _ = join(t_near, t_far, w_far_c)
    c_near = shift(t_near, "c", 1)
    c_far = shift(t_far, "c", 1)
    texts = jnp.concatenate([t_near[:512], t_far, t_near[512:], c_near[:512], c_far, c_near[512:]], 0)

    def embed(rows):
        raw = jnp.dot(rows, weight, preferred_element_type=F32)
        unit, norm = unit_rows(raw)
        return unit.astype(BF), norm

    emb, norm = embed(images)

    def pair(e, t):
        logits = mult * lax.dot_general(e, t, (((1,), (1,)), ((), ())), preferred_element_type=F32) + bias
        return (jax.nn.sigmoid(logits) * mult).astype(BF)

    def pair_own(e, t):
        logits = mult * lax.dot_general(e, t, (((1,), (1,)), ((), ())), preferred_element_type=F32) + bias
        row = lax.broadcasted_iota(jnp.int32, logits.shape, 0)
        col = lax.broadcasted_iota(jnp.int32, logits.shape, 1)
        sign = jnp.where(row == col, 1.0, -1.0)
        return (-sign * jax.nn.sigmoid(-sign * logits) * mult).astype(BF)

    def back_t(pg, e):
        return lax.dot_general(pg, e, (((0,), (0,)), ((), ())), preferred_element_type=F32)

    def project(g, e, n):
        return unit_backward(g, e.astype(F32), n)

    grads = lax.dynamic_update_slice(pair(emb, texts), pair_own(emb[:128], texts[:128]), (0, 0))
    r0 = project(jnp.dot(grads[:512], texts, preferred_element_type=F32), emb[:512], norm[:512]).astype(BF)
    r1 = project(jnp.dot(grads[512:], texts, preferred_element_type=F32), emb[512:], norm[512:]).astype(BF)

    r1_here = shift(r1, "yh", 1)
    gw = (back_t(images[:512], r0) + back_t(images[512:], r1)).astype(BF)
    keep, send = spread(pos, gw)
    send = shift(send, "c", 1)
    gt_send = back_t(grads[:, 1024:], emb)
    keep, send, gt_send = join(keep, send, gt_send)
    gt_send = gt_send.astype(BF)

    s, grads = join((keep.astype(F32) + send.astype(F32)).astype(BF), grads)
    s = near_sum(s, "x", 160)
    gt = back_t(grads[:, :1024], emb)
    gt = gt + shift(gt_send, "c", 1).astype(F32)
    gt = ring_first([rows_of(gt, k, 256) for k in range(4)], "z")
    s, gt, r0 = join(s, gt, r0)

    s = (s[:80] + shift(s[80:].astype(BF), "yh", 1).astype(F32)).astype(BF)
    s = (s.astype(F32) + shift(s, "yl", 1).astype(F32)).astype(BF)
    gt = ring_second(*gt, "z")
    r0 = r0.astype(F32) + r1_here.astype(F32)
    raw_grad = near_sum(r0.astype(BF), "x").astype(BF)
    gt, gt_y, s, raw_grad = join(gt[:128], gt[128:].astype(BF), s, raw_grad)

    text_grad = gt + shift(gt_y, "yl", 1).astype(F32)
    text_unit, text_norm = unit_rows(text_feats.astype(F32))
    grad_text = unit_backward(text_grad, text_unit, text_norm)
    zp, zm, zf = shift(s, "z", 1), shift(s, "z", -1), shift(s, "z", 2)
    s = ((s.astype(F32) + zf.astype(F32)) + (zp.astype(F32) + zm.astype(F32))).astype(BF)
    o = shift(s, "c", 1)
    lo = jnp.where(core == 0, s, o)
    hi = jnp.where(core == 0, o, s)
    grad_weight = jnp.concatenate([lo, hi[16:]], 0).astype(F32)
    grad_pooled = lax.dot_general(raw_grad, weight, (((1,), (1,)), ((), ())), preferred_element_type=F32).astype(BF)
    return (grad_text, grad_pooled, grad_weight)


def solution(mesh):
    placed = (P(AXES, None), P(AXES, None), P("fsdp", None), P(), P())
    return jax.shard_map(
        local,
        mesh=mesh,
        in_specs=placed,
        out_specs=(P(AXES, None), P(AXES, None), P("fsdp", None)),
        check_vma=False,
    )
```

```python
import functools

import jax
import jax.numpy as jnp
from jax import lax
from jax.experimental import pallas as pl
from jax.experimental.pallas import tpu as pltpu
from jax.sharding import PartitionSpec as P

epsilon = 1e-06
BF = jnp.bfloat16
F32 = jnp.float32
AXES = ("dp", "fsdp")
SIZES = {"z": 4, "yl": 2, "c": 2, "x": 4, "yh": 2}


def place_of(i):
    dp, fs = divmod(i, 8)
    return {"z": dp // 4, "yl": dp // 2 % 2, "c": dp % 2, "x": fs // 2, "yh": fs % 2}


def index_of(p):
    return (p["z"] * 4 + p["yl"] * 2 + p["c"]) * 8 + p["x"] * 2 + p["yh"]


def shift(value, axis, by):
    pairs = []
    for i in range(128):
        p = place_of(i)
        p[axis] = (p[axis] + by) % SIZES[axis]
        pairs.append((i, index_of(p)))
    return lax.ppermute(value, AXES, pairs)


def join(*values):
    return lax.optimization_barrier(values)


def both_ways(block, axis):
    return shift(block, axis, -1), shift(block, axis, 1)


def rows_of(v, k, n=128):
    return v[k * n:(k + 1) * n]


def ring_first(v, axis):
    half = v[0].shape[0] // 2
    far = v[2].astype(BF)
    a = shift(far[:half], axis, 1).astype(F32)
    b = shift(far[half:], axis, -1).astype(F32)
    plus = jnp.concatenate([v[1][:half] + a, v[1][half:]], 0).astype(BF)
    minus = jnp.concatenate([v[3][:half], v[3][half:] + b], 0).astype(BF)
    return v[0], plus, minus


def ring_second(own, plus, minus, axis):
    return own + (shift(plus, axis, 1).astype(F32) + shift(minus, axis, -1).astype(F32))


def near_sum(v, axis, n=128):
    r1 = shift(rows_of(v, 1, n), axis, 1).astype(F32)
    r2 = shift(rows_of(v, 2, n), axis, 2).astype(F32)
    r3 = shift(rows_of(v, 3, n), axis, -1).astype(F32)
    return (rows_of(v, 0, n).astype(F32) + r2) + (r1 + r3)


def unit_rows(values):
    norms = jnp.sqrt(jnp.sum(values * values, axis=-1, keepdims=True) + epsilon)
    return (values / norms, norms)


def unit_backward(upstream, unit, norms):
    return (upstream - unit * jnp.sum(unit * upstream, axis=-1, keepdims=True)) / norms


def block_row(pos, dx, dy):
    x, yh = pos[0], pos[1]
    return (lax.rem(x + dx, 4) * 2 + lax.rem(yh + dy, 2)) * 144


def prepare_kernel(weight, pooled, text, own, emb, held, sems):
    core = lax.rem(lax.axis_index("dp"), 2)
    share = weight.at[pl.ds(pl.multiple_of(core * 64, 16), 80)]
    copies = [
        pltpu.make_async_copy(text, held, sems.at[0]),
        pltpu.make_async_copy(share, own.at[pl.ds(0, 80)], sems.at[1]),
        pltpu.make_async_copy(pooled, own.at[pl.ds(80, 128)], sems.at[2]),
    ]
    for copy in copies:
        copy.start()
    for copy in copies:
        copy.wait()
    values = held[...].astype(F32)
    emb[...] = (values / jnp.sqrt(jnp.sum(values * values, axis=-1, keepdims=True) + epsilon)).astype(BF)


def prepare(weight, pooled, text):
    return pl.pallas_call(
        prepare_kernel,
        out_shape=[jax.ShapeDtypeStruct((208, 1152), BF), jax.ShapeDtypeStruct((128, 1152), BF)],
        in_specs=[pl.BlockSpec(memory_space=pl.ANY)] * 3,
        out_specs=[pl.BlockSpec(memory_space=pltpu.VMEM)] * 2,
        scratch_shapes=[pltpu.VMEM((128, 1152), BF), pltpu.SemaphoreType.DMA((3,))],
        compiler_params=pltpu.CompilerParams(vmem_limit_bytes=63 * 2**20),
    )(weight, pooled, text)


def assemble_kernel(pos, near, far, near_c, far_c, out):
    c = pos[2]
    for dx in range(4):
        for dy in range(2):
            own, oth, k = (far, far_c, 96 * dy) if dx == 2 else (near, near_c, ((0, 1, 2, 2)[dx] * 2 + dy) * 80)
            base = block_row(pos, dx, dy)
            out[pl.ds(pl.multiple_of(base + c * 64, 16), 80), :] = own[pl.ds(k, 80), :]
            out[pl.ds(pl.multiple_of(base + 80 * (1 - c), 16), 64), :] = oth[pl.ds(pl.multiple_of(k + 16 * (1 - c), 16), 64), :]


def assemble(pos, *parts):
    return pl.pallas_call(
        assemble_kernel,
        out_shape=jax.ShapeDtypeStruct((1152, 1152), BF),
        in_specs=[pl.BlockSpec(memory_space=pltpu.SMEM)] + [pl.BlockSpec(memory_space=pltpu.VMEM)] * 4,
        out_specs=pl.BlockSpec(memory_space=pltpu.VMEM),
        compiler_params=pltpu.CompilerParams(vmem_limit_bytes=32 * 2**20),
    )(pos, *parts)


def give_kernel(pos, whole, send):
    c = pos[2]
    for dx in range(4):
        for dy in range(2):
            row = pl.multiple_of(block_row(pos, dx, dy) + (1 - c) * 64, 16)
            send[pl.ds((dx * 2 + dy) * 80, 80), :] = whole[pl.ds(row, 80), :]


def take_kernel(pos, whole, got, out):
    c = pos[2]
    for dx in range(4):
        for dy in range(2):
            row = pl.multiple_of(block_row(pos, dx, dy) + c * 64, 16)
            at = pl.ds((dx * 2 + dy) * 80, 80)
            out[at, :] = (whole[pl.ds(row, 80), :].astype(F32) + got[at, :].astype(F32)).astype(BF)


def by_blocks(kernel, pos, *arrays):
    return pl.pallas_call(
        kernel,
        out_shape=jax.ShapeDtypeStruct((640, 1152), BF),
        in_specs=[pl.BlockSpec(memory_space=pltpu.SMEM)] + [pl.BlockSpec(memory_space=pltpu.VMEM)] * len(arrays),
        out_specs=pl.BlockSpec(memory_space=pltpu.VMEM),
        compiler_params=pltpu.CompilerParams(vmem_limit_bytes=32 * 2**20),
    )(pos, *arrays)


def local(pooled, text_feats, out_weight, logit_scale, logit_bias):
    dp = lax.axis_index("dp")
    fs = lax.axis_index("fsdp")
    core = dp % 2
    pos = jnp.stack([fs // 2, fs % 2, core]).astype(jnp.int32)
    mult = logit_scale[0]
    bias = logit_bias[0]

    own, text_emb = prepare(out_weight, pooled, text_feats)
    oth = shift(own, "yh", 1)
    own_p, own_m = both_ways(own, "x")
    oth_p, oth_m = both_ways(oth, "x")
    far_a = shift(jnp.concatenate([own_m[:96], oth_m[:96]], 0), "x", 1)
    far_b = shift(jnp.concatenate([own_p[96:], oth_p[96:]], 0), "x", -1)
    w_near = jnp.concatenate([v[:80] for v in (own, oth, own_p, oth_p, own_m, oth_m)], 0)
    w_far_c = shift(far_a, "c", 1)
    weight = assemble(pos, w_near, far_a, shift(w_near, "c", 1), w_far_c)
    images = jnp.concatenate([
        pooled, own_p[80:], far_a[80:96], far_b[:112], own_m[80:],
        oth[80:], oth_p[80:], far_a[176:], far_b[112:], oth_m[80:]], 0)

    text_own, _ = join(text_emb, oth)
    text_oth = shift(text_own, "yl", 1)
    t_p, t_m = both_ways(text_emb, "z")
    u_p, u_m = both_ways(text_oth, "z")
    fa = shift(jnp.concatenate([t_m[:64], u_m[:64]], 0), "z", 1)
    fb = shift(jnp.concatenate([t_p[64:], u_p[64:]], 0), "z", -1)
    t_near = jnp.concatenate([text_emb, text_oth, t_p, u_p, t_m, u_m], 0)
    t_far = jnp.concatenate([fa[:64], fb[:64], fa[64:], fb[64:]], 0)
    t_near, t_far, _ = join(t_near, t_far, w_far_c)
    c_near = shift(t_near, "c", 1)
    c_far = shift(t_far, "c", 1)
    texts = jnp.concatenate([t_near[:512], t_far, t_near[512:], c_near[:512], c_far, c_near[512:]], 0)

    def embed(rows):
        raw = jnp.dot(rows, weight, preferred_element_type=F32)
        unit, norm = unit_rows(raw)
        return unit.astype(BF), norm

    emb, norm = embed(images)

    def pair(e, t):
        logits = mult * lax.dot_general(e, t, (((1,), (1,)), ((), ())), preferred_element_type=F32) + bias
        return (jax.nn.sigmoid(logits) * mult).astype(BF)

    def pair_own(e, t):
        logits = mult * lax.dot_general(e, t, (((1,), (1,)), ((), ())), preferred_element_type=F32) + bias
        row = lax.broadcasted_iota(jnp.int32, logits.shape, 0)
        col = lax.broadcasted_iota(jnp.int32, logits.shape, 1)
        sign = jnp.where(row == col, 1.0, -1.0)
        return (-sign * jax.nn.sigmoid(-sign * logits) * mult).astype(BF)

    def back_t(pg, e):
        return lax.dot_general(pg, e, (((0,), (0,)), ((), ())), preferred_element_type=F32)

    def project(g, e, n):
        return unit_backward(g, e.astype(F32), n)

    grads = lax.dynamic_update_slice(pair(emb, texts), pair_own(emb[:128], texts[:128]), (0, 0))
    r0 = project(jnp.dot(grads[:512], texts, preferred_element_type=F32), emb[:512], norm[:512]).astype(BF)
    r1 = project(jnp.dot(grads[512:], texts, preferred_element_type=F32), emb[512:], norm[512:]).astype(BF)

    r1_here = shift(r1, "yh", 1)
    gw = (back_t(images[:512], r0) + back_t(images[512:], r1)).astype(BF)
    send = shift(by_blocks(give_kernel, pos, gw), "c", 1)
    gt_send = back_t(grads[:, 1024:], emb)
    send, gt_send = join(send, gt_send)
    gt_send = gt_send.astype(BF)

    s, grads = join(by_blocks(take_kernel, pos, gw, send), grads)
    s = near_sum(s, "x", 160)
    gt = back_t(grads[:, :1024], emb)
    gt = gt + shift(gt_send, "c", 1).astype(F32)
    gt = ring_first([rows_of(gt, k, 256) for k in range(4)], "z")
    s, gt, r0 = join(s, gt, r0)

    s = (s[:80] + shift(s[80:].astype(BF), "yh", 1).astype(F32)).astype(BF)
    s = (s.astype(F32) + shift(s, "yl", 1).astype(F32)).astype(BF)
    gt = ring_second(*gt, "z")
    r0 = r0.astype(F32) + r1_here.astype(F32)
    raw_grad = near_sum(r0.astype(BF), "x").astype(BF)
    gt, gt_y, s, raw_grad = join(gt[:128], gt[128:].astype(BF), s, raw_grad)

    text_grad = gt + shift(gt_y, "yl", 1).astype(F32)
    text_unit, text_norm = unit_rows(text_feats.astype(F32))
    grad_text = unit_backward(text_grad, text_unit, text_norm)
    zp, zm, zf = shift(s, "z", 1), shift(s, "z", -1), shift(s, "z", 2)
    s = ((s.astype(F32) + zf.astype(F32)) + (zp.astype(F32) + zm.astype(F32))).astype(BF)
    o = shift(s, "c", 1)
    lo = jnp.where(core == 0, s, o)
    hi = jnp.where(core == 0, o, s)
    grad_weight = jnp.concatenate([lo, hi[16:]], 0).astype(F32)
    grad_pooled = lax.dot_general(raw_grad, weight, (((1,), (1,)), ((), ())), preferred_element_type=F32).astype(BF)
    return (grad_text, grad_pooled, grad_weight)


def solution(mesh):
    placed = (P(AXES, None), P(AXES, None), P("fsdp", None), P(), P())
    return jax.shard_map(
        local,
        mesh=mesh,
        in_specs=placed,
        out_specs=(P(AXES, None), P(AXES, None), P("fsdp", None)),
        check_vma=False,
    )
```
